128 devices in a mesh: blk: 4 (over z), dom: 32 (over x, y, core).
Axes of the slice: x: 4, y: 4, z: 4, core: 2. Of those that a mesh axis runs over, the one named last changes fastest.
Arguments:
- tiles: bfloat16 [49152, 128, 128], P(('blk', 'dom')), may hold values from -0.109375 to 0.109375
- tile_rows: int32 [49152], P(('blk', 'dom')), may hold values from 0 to 511, as said below
- tile_cols: int32 [49152], P(('blk', 'dom')), may hold values from 0 to 511, as said below
- tile_counts: int32 [128], P(('blk', 'dom')), may hold values from 32 to 384, as said below
- loads_in: bfloat16 [65536, 512], P(('blk', 'dom')), may hold values from -6 to 6
Outputs:
- response: float32 [65536, 512], P(('blk', 'dom'))
The draws below stay inside these ranges and needn't reach their ends.
Inputs may be any that keep to these rules, and one draw needn't show every extreme that they name: `tile_counts`: one device has exactly 384 live slots in every draw. `tile_rows`: for the device at index b of blk, every live slot names a block row in [b * 128, (b + 1) * 128); within a device the live slots' block rows never fall from one slot to the next. Slots at or past a device's count are ignored. `tile_cols`: for the device at index d of dom, every slot names a block column c such that c // 4 equals d modulo the number of devices along dom. (row, column) pairs may repeat; repeated tiles add.
All inputs are finite; a program needn't handle non-finite values.
Results may differ from the reference program's by a relative error of at most 0.0003.
Values may be sent and summed in bfloat16 or wider, within the bound.
No kernel may reach another device: no remote copies, remote signals or barrier semaphores. Data moves between devices by JAX's collectives and lax.ppermute only.
A program may use at most 192 MiB of HBM per device.

```python
import jax
import jax.numpy as jnp
from jax import lax

BLK = 128
LOADS = 512
PB = 4
TCAP = 384
RGROUP = 128
ORDER = 65536
TILES = 49152
N_DOM = 32


def shared_counts(key):
    devices = TILES // TCAP
    sub = jax.random.fold_in(key, 7)
    first_key, second_key = jax.random.split(sub)
    counts = jax.random.randint(first_key, (devices,), 8 * PB, TCAP + 1)
    busiest = jax.random.randint(second_key, (), 0, devices)
    return jnp.where(jnp.arange(devices) == busiest, TCAP, counts).astype(jnp.int32)


def draw_tile_counts(key, part):
    return shared_counts(key)


def draw_tile_rows(key, part):
    devices = TILES // TCAP
    n_dom = RGROUP // PB
    counts = shared_counts(key)
    sub = jax.random.fold_in(key, 11)
    raw = jax.random.randint(sub, (devices, TCAP), 0, RGROUP)
    slots = jnp.arange(TCAP)[None, :]
    raw = jnp.where(slots < counts[:, None], raw, RGROUP - 1)
    ordered = jnp.sort(raw, axis=1)
    group = (jnp.arange(devices) // n_dom)[:, None]
    return (ordered + group * RGROUP).reshape(TILES).astype(jnp.int32)


def draw_tile_cols(key, part):
    devices = TILES // TCAP
    n_dom = RGROUP // PB
    n_blk = devices // n_dom
    sub = jax.random.fold_in(key, 13)
    first_key, second_key = jax.random.split(sub)
    cycle_pos = jax.random.randint(first_key, (devices, TCAP), 0, n_blk)
    inner = jax.random.randint(second_key, (devices, TCAP), 0, PB)
    dom_pos = (jnp.arange(devices) % n_dom)[:, None]
    columns = (cycle_pos * n_dom + dom_pos) * PB + inner
    return columns.reshape(TILES).astype(jnp.int32)


def block_levels(stream_key, extent, cuts, smallest, high):
    gain = 1.0
    for axis_at, shards_of in cuts:
        steps = jax.random.uniform(jax.random.fold_in(jax.random.fold_in(stream_key, 6), axis_at), (shards_of,), jnp.float32, smallest / len(cuts), high / len(cuts))
        gain = gain * jnp.repeat(jnp.exp(steps), extent[axis_at] // shards_of).reshape((-1,) + (1,) * (len(extent) - 1 - axis_at))
    return gain


def normal_values(stream_key, dims, width, limit, pieces=(), kind=jnp.bfloat16):
    values = width * jax.random.normal(stream_key, dims, jnp.float32)
    if pieces:
        values = values * block_levels(stream_key, dims, pieces, -0.22, 0.18)
    return jnp.clip(values, -limit, limit).astype(kind)


def setup_inputs(seed: int = 0) -> dict:
    keys = jax.random.split(jax.random.key(seed), 6)
    return {
        "tiles": normal_values(keys[0], (TILES, BLK, BLK), (24 * BLK) ** -0.5, 0.109375, ((0, 128),)),
        "tile_rows": draw_tile_rows(jax.random.fold_in(keys[5], 71), 0),
        "tile_cols": draw_tile_cols(jax.random.fold_in(keys[5], 71), 0),
        "tile_counts": draw_tile_counts(jax.random.fold_in(keys[5], 71), 0),
        "loads_in": normal_values(keys[4], (ORDER, LOADS), 1.0, 6.0, ((0, 128),)),
    }


def reference(tiles, tile_rows, tile_cols, tile_counts, loads_in):
    slots = tiles.shape[0]
    devices = tile_counts.shape[0]
    tcap = slots // devices
    blk = tiles.shape[1]
    loads = loads_in.shape[1]
    nblocks = loads_in.shape[0] // blk
    xblocks = loads_in.astype(jnp.float32).reshape(nblocks, blk, loads)

    def step(total, device):
        begin = (device * tcap).astype(jnp.int32)
        base = ((device // N_DOM) * RGROUP).astype(jnp.int32)
        tile_group = lax.dynamic_slice_in_dim(tiles, begin, tcap, 0).astype(jnp.float32)
        rows = lax.dynamic_slice_in_dim(tile_rows, begin, tcap, 0) - base
        cols = lax.dynamic_slice_in_dim(tile_cols, begin, tcap, 0)
        alive = jnp.arange(tcap, dtype=jnp.int32) < tile_counts[device]
        xgroup = jnp.take(xblocks, cols, axis=0)
        prods = jnp.einsum("gij,gjc->gic", tile_group, xgroup, precision=lax.Precision.HIGHEST)
        target = jnp.where(alive, rows, RGROUP).astype(jnp.int32)
        partial_value = jnp.zeros((RGROUP, blk, loads), jnp.float32).at[target].add(prods, mode="drop")
        current = lax.dynamic_slice_in_dim(total, base, RGROUP, 0)
        total = lax.dynamic_update_slice_in_dim(total, current + partial_value, base, 0)
        return total, None

    start = jnp.zeros((nblocks, blk, loads), jnp.float32)
    total, _ = lax.scan(step, start, jnp.arange(devices, dtype=jnp.int32))
    return total.reshape(nblocks * blk, loads)
```

```python
import functools

import jax
import jax.numpy as jnp
from jax import lax
from jax.experimental import pallas as pl
from jax.experimental.pallas import tpu as pltpu
from jax.sharding import PartitionSpec as P

CHUNKS = 2
REL = (2, 1, 3, 0)
UNROLL = 8
VMEM_LIMIT = 16 * 2**20
ORDER = (
    ("far", 0), ("rest", 0), ("ring1", 0), ("far", 1), ("rest", 1), ("ring1", 1), ("ring2", 0), ("ring2", 1), ("ring3", 0), ("ring3", 1),
)
FINE = 16.0
TOP = 32752.0
GROUP_FLOPS = 4_400_000_000


def tables(tile_rows, tile_cols, tile_counts, pb, n_blk, n_dom):
    slots = tile_rows.shape[0]
    rgroup = pb * n_dom
    d = lax.axis_index("dom")
    px, py, core = d // 8, (d // 2) % 4, d % 2
    rel = jnp.array(REL, jnp.int32)

    def starts(core):
        u, v = jnp.where(core == 0, px, py), jnp.where(core == 0, py, px)
        q, p = (u + rel[:, None]) % 4, (v + rel[None, :]) % 4
        return jnp.where(core == 0, (q * 4 + p) * 2, (p * 4 + q) * 2 + 1).reshape(-1)

    order = jnp.concatenate([starts(1 - core), starts(core)])
    edge = jnp.arange(rgroup, dtype=jnp.int32)
    group = jnp.arange(n_dom, dtype=jnp.int32)
    pos = jnp.sum(jnp.where(order[None, :] == edge[:, None] // pb, group[None, :] * pb, 0), axis=1) + edge % pb
    slot = jnp.arange(slots, dtype=jnp.int32)
    rows = jnp.where(slot < tile_counts[0], tile_rows - lax.axis_index("blk") * rgroup, rgroup)
    behind = (tile_cols // pb // n_dom - lax.axis_index("blk")) % n_blk
    xcol = jnp.clip(behind * pb + tile_cols % pb, 0, n_blk * pb - 1)
    ptr = jnp.sum((rows[None, :] < edge[:, None]).astype(jnp.int32), axis=1)
    num = jnp.sum((rows[None, :] == edge[:, None]).astype(jnp.int32), axis=1)
    half = (num + 1) // 2
    off = jnp.sum(jnp.where(pos[None, :] < pos[:, None], half[None, :], 0), axis=1)
    bound = jnp.arange(n_dom + 1, dtype=jnp.int32) * pb
    bound = jnp.sum(jnp.where(pos[None, :] < bound[:, None], half[None, :], 0), axis=1)
    item = jnp.arange((slots + rgroup) // 2 + UNROLL, dtype=jnp.int32)
    hot = (off[None, :] <= item[:, None]) & (item[:, None] < (off + half)[None, :])
    pick = lambda v: jnp.sum(jnp.where(hot, v[None, :], 0), axis=1)
    first = jnp.clip(pick(ptr - 2 * off) + 2 * item, 0, slots - 1)
    paired = first + 1 < pick(ptr + num)
    second = jnp.where(paired, first + 1, first)
    at = lambda t: jnp.sum(jnp.where(t[:, None] == slot[None, :], xcol[None, :], 0), axis=1)
    parts = dict(bound=bound, row=pick(pos), first=first, second=second, xa=at(first))
    parts["xb"] = jnp.where(paired, at(second), n_blk * pb)
    where, n = {}, 0
    for k, v in parts.items():
        where[k] = n
        n += v.shape[0]
    return where, jnp.concatenate(list(parts.values())).astype(jnp.int32)


def scale_of(msg, groups, g):
    blk = msg[pl.ds(groups * 512, 16), :].astype(jnp.int32).astype(jnp.float32)
    at = lax.broadcasted_iota(jnp.int32, blk.shape, 0)
    e = jnp.sum(jnp.where(at == g, blk, 0.0), axis=0, keepdims=True)
    return jnp.exp2(e * (1 / FINE)) * (1 / TOP)


def loop(count, body):
    if count == 1:
        body(0)
    else:
        lax.fori_loop(0, count, lambda k, _: (body(k), 0)[1], 0)


def kernel(where, base, total, segs, nin, nwait, outs, tab, tiles, x, *refs):
    ins, out_refs = refs[:nin], refs[nin + nwait : nin + nwait + len(outs)]
    acc, sc = refs[nin + nwait + len(outs) :]
    width = x.shape[-1]

    for first, count, adds, _, _ in segs:

        def begin(k):
            scales = [scale_of(ins[i], n, m + k) for i, n, m in adds]
            for i in range(4):
                value = None
                for (ref, _, m), s in zip(adds, scales):
                    at = pl.ds(pl.multiple_of((m + k) * 512 + i * 128, 128), 128)
                    part = ins[ref][at, :].astype(jnp.int32).astype(jnp.float32) * s
                    value = part if value is None else value + part
                acc[(first + k) * 4 + i] = jnp.zeros(acc.shape[1:], jnp.float32) if value is None else value

        loop(count, begin)

    lo, hi = tab[where["bound"] + base], tab[where["bound"] + base + total]

    def body(j, _):
        done = []
        for n in range(UNROLL):
            t = lo + j * UNROLL + n
            row = jnp.where(t < hi, tab[where["row"] + t] - 4 * base, 4 * total)
            lhs = jnp.concatenate([tiles[tab[where["first"] + t]], tiles[tab[where["second"] + t]]], axis=1)
            rhs = jnp.concatenate([x[tab[where["xa"] + t]], x[tab[where["xb"] + t]]], axis=0)
            done.append((row, jnp.dot(lhs, rhs, preferred_element_type=jnp.float32)))
        for row, value in done:
            acc[row] += value
        return 0

    lax.fori_loop(0, (hi - lo + UNROLL - 1) >> (UNROLL.bit_length() - 1), body, 0)

    sublane = lax.broadcasted_iota(jnp.int32, (16, width), 0)
    for o, (_, quant) in enumerate(outs):
        if quant:
            sc[o] = jnp.zeros(sc.shape[1:], jnp.int32)
    for first, count, _, o, place in segs:

        def finish(k):
            out = out_refs[o]
            terms = [acc.at[(first + k) * 4 + i] for i in range(4)]
            if not outs[o][1]:
                for i in range(4):
                    out[pl.ds(i * 128, 128), :] = terms[i][...]
                return
            top = functools.reduce(jnp.maximum, [jnp.max(jnp.abs(t[...]), axis=0, keepdims=True) for t in terms])
            e = jnp.ceil(FINE * jnp.log2(jnp.maximum(top, 1e-30)))
            inv = jnp.exp2(e * (-1 / FINE)) * TOP
            for i in range(4):
                at = pl.ds(pl.multiple_of((place + k) * 512 + i * 128, 128), 128)
                out[at, :] = jnp.round(terms[i][...] * inv).astype(jnp.int32).astype(jnp.int16)
            sc[o] = jnp.where(sublane == place + k, e.astype(jnp.int32), sc[o])

        loop(count, finish)
    for o, (groups, quant) in enumerate(outs):
        if quant:
            out_refs[o][pl.ds(groups * 512, 16), :] = sc[o].astype(jnp.int16)


def products(name, where, tab, tiles, x, base, total, segs, ins, outs, wait):
    width = x.shape[-1]
    blk = tiles.shape[1]
    smem, vmem = pl.BlockSpec(memory_space=pltpu.SMEM), pl.BlockSpec(memory_space=pltpu.VMEM)
    shapes = [
        jax.ShapeDtypeStruct((n * 512 + 16, width), jnp.int16) if quant else jax.ShapeDtypeStruct((512, width), jnp.float32)
        for n, quant in outs
    ]
    return pl.pallas_call(
        functools.partial(kernel, where, base, total, segs, len(ins), len(wait), outs),
        out_shape=shapes,
        in_specs=[smem] + [vmem] * (2 + len(ins)) + [pl.BlockSpec(memory_space=pl.ANY)] * len(wait),
        out_specs=[vmem] * len(outs),
        scratch_shapes=[
            pltpu.VMEM((4 * total + 1, blk, width), jnp.float32),
            pltpu.VMEM((len(outs), 16, width), jnp.int32),
        ],
        compiler_params=pltpu.CompilerParams(vmem_limit_bytes=VMEM_LIMIT),
        cost_estimate=pl.CostEstimate(flops=total * GROUP_FLOPS, bytes_accessed=1000, transcendentals=0),
        name=name,
    )(tab, tiles, x, *ins, *wait)


def join_kernel(n, nwait, *refs):
    out, at = refs[-1], 0
    for part in refs[:n]:
        out[pl.ds(at, part.shape[0])] = part[...]
        at += part.shape[0]
    out[pl.ds(at, out.shape[0] - at)] = jnp.zeros((out.shape[0] - at, *out.shape[1:]), out.dtype)


def join(name, parts, blk, wait):
    parts = [p.reshape(-1, blk, p.shape[-1]) for p in parts]
    total = sum(p.shape[0] for p in parts)
    return pl.pallas_call(
        functools.partial(join_kernel, len(parts), len(wait)),
        out_shape=jax.ShapeDtypeStruct((total + 1, *parts[0].shape[1:]), parts[0].dtype),
        in_specs=[pl.BlockSpec(memory_space=pltpu.VMEM)] * len(parts) + [pl.BlockSpec(memory_space=pl.ANY)] * len(wait),
        out_specs=pl.BlockSpec(memory_space=pltpu.VMEM),
        compiler_params=pltpu.CompilerParams(vmem_limit_bytes=VMEM_LIMIT),
        cost_estimate=pl.CostEstimate(flops=1000, bytes_accessed=1000, transcendentals=0),
        name=name,
    )(*parts, *wait)


def hold_kernel(src, dst, sem):
    copy = pltpu.make_async_copy(src, dst, sem)
    copy.start()
    copy.wait()


def hold(value):
    return pl.pallas_call(
        hold_kernel,
        out_shape=jax.ShapeDtypeStruct(value.shape, value.dtype),
        in_specs=[pl.BlockSpec(memory_space=pltpu.HBM)],
        out_specs=pl.BlockSpec(memory_space=pltpu.VMEM),
        scratch_shapes=[pltpu.SemaphoreType.DMA],
        compiler_params=pltpu.CompilerParams(vmem_limit_bytes=VMEM_LIMIT),
        cost_estimate=pl.CostEstimate(flops=GROUP_FLOPS, bytes_accessed=1000, transcendentals=0),
        name="hold",
    )(value)


def add_up_kernel(n, nwait, *refs):
    out = refs[-1]
    for j in range(n):
        own, *got = refs[4 * j : 4 * j + 4]
        width = own.shape[1]
        scales = [scale_of(m, 1, 0) for m in got]

        def some(i, _):
            at = pl.ds(pl.multiple_of(i * 128, 128), 128)
            value = own[at, :]
            for m, s in zip(got, scales):
                value = value + m[at, :].astype(jnp.int32).astype(jnp.float32) * s
            out[at, j * width : (j + 1) * width] = value
            return 0

        lax.fori_loop(0, own.shape[0] // 128, some, 0)


def add_up(parts, wait):
    rows, width = parts[0][0].shape
    flat = [p for part in parts for p in part]
    return pl.pallas_call(
        functools.partial(add_up_kernel, len(parts), len(wait)),
        out_shape=jax.ShapeDtypeStruct((rows, width * len(parts)), jnp.float32),
        in_specs=[pl.BlockSpec(memory_space=pltpu.VMEM)] * len(flat) + [pl.BlockSpec(memory_space=pl.ANY)] * len(wait),
        out_specs=pl.BlockSpec(memory_space=pltpu.VMEM),
        compiler_params=pltpu.CompilerParams(vmem_limit_bytes=VMEM_LIMIT),
        name="add_up",
    )(*flat, *wait)


def shards(tiles, tile_rows, tile_cols, tile_counts, loads_in):
    blk, loads = tiles.shape[1], loads_in.shape[1]
    pb = loads_in.shape[0] // blk
    n_blk, n_dom = lax.axis_size("blk"), lax.axis_size("dom")
    where, tab = tables(tile_rows, tile_cols, tile_counts, pb, n_blk, n_dom)
    width = loads // CHUNKS

    place = lambda x, y, c: (x % 4 * 4 + y % 4) * 2 + c
    every = [(x, y, c) for x in range(4) for y in range(4) for c in range(2)]
    pair = [(place(x, y, c), place(x, y, 1 - c)) for x, y, c in every]
    along = lambda k, axis: [
        (place(x, y, c), place(x + k, y, c) if c == axis else place(x, y + k, c)) for x, y, c in every
    ]
    send = lambda value, pairs: lax.ppermute(value, "dom", pairs)

    tiles = hold(tiles)
    ring = lambda k: [(i, (i - k) % n_blk) for i in range(n_blk)]
    parts = []
    for j in range(CHUNKS):
        part = loads_in[:, j * width : (j + 1) * width]
        others = [lax.ppermute(part, "blk", ring(k)) for k in (1, n_blk - 1, *range(2, n_blk - 1))]
        others.insert(n_blk - 2, others.pop(1))
        parts.append([part, *others])
    last, xs = [], {}

    def run(name, j, wait=(), **how):
        if j not in xs:
            xs[j] = join(f"join_{j}", parts[j], blk, list(last))
        value = products(f"{name}_{j}", where, tab, tiles, xs[j], wait=[*last, *wait], **how)
        last[:] = [value[-1]]
        return value

    kept = [{} for _ in range(CHUNKS)]

    def far(j, k):
        [a] = run("far", j, base=0, total=4, segs=[(0, 4, [], 0, 0)], ins=[], outs=[(4, True)])
        k["p1"] = send(a, pair)

    def ring1(j, k):
        h1, h2 = run(
            "ring1", j, wait=kept[j - 1]["r"] if j else (), base=16, total=4, ins=[k["p1"]], outs=[(2, True), (2, True)],
            segs=[(0, 2, [(0, 4, 0)], 0, 0), (2, 2, [(0, 4, 2)], 1, 0)],
        )
        k["r"] = send(h1, along(1, 0)), send(h2, along(-1, 0))

    def rest(j, k):
        [a] = run("rest", j, base=4, total=12, segs=[(0, 12, [], 0, 0)], ins=[], outs=[(12, True)])
        k["p2"] = send(a, pair)

    def ring2(j, k):
        m1, m2 = run(
            "ring2", j, base=20, total=8, ins=[k["p2"], *k["r"]], outs=[(4, True), (4, True)],
            segs=[
                (0, 2, [(0, 12, 0), (1, 2, 0)], 0, 0),
                (2, 2, [(0, 12, 2)], 0, 2),
                (4, 2, [(0, 12, 4)], 1, 0),
                (6, 2, [(0, 12, 6), (2, 2, 0)], 1, 2),
            ],
        )
        k["n"] = send(m1, along(1, 0)), send(m2, along(-1, 0))

    def ring3(j, k):
        t0, t1, t2, own = run(
            "ring3", j, base=28, total=4, ins=[k["p2"], *k["n"]], outs=[(1, True), (1, True), (1, True), (1, False)],
            segs=[(g, 1, [(0, 12, 8 + g), (1, 4, g), (2, 4, g)], g, 0) for g in range(4)],
        )
        k["t"] = own, [send(t0, along(2, 1)), send(t1, along(1, 1)), send(t2, along(-1, 1))]

    for step, j in ORDER:
        dict(far=far, ring1=ring1, rest=rest, ring2=ring2, ring3=ring3)[step](j, kept[j])
    return add_up([[k["t"][0], *k["t"][1]] for k in kept], last)


def solution(mesh):
    in_specs = (
        P(("blk", "dom"), None, None),
        P(("blk", "dom")),
        P(("blk", "dom")),
        P(("blk", "dom")),
        P(("blk", "dom"), None),
    )
    out_specs = P(("blk", "dom"), None)
    return jax.shard_map(shards, mesh=mesh, in_specs=in_specs, out_specs=out_specs, check_vma=False)
```

```python
import functools

import jax
import jax.numpy as jnp
from jax import lax
from jax.experimental import pallas as pl
from jax.experimental.pallas import tpu as pltpu
from jax.sharding import PartitionSpec as P

SPLIT = (1, 1)
CHUNKS = len(SPLIT)
REL = (2, 1, 3, 0)
UNROLL = 8
VMEM_LIMIT = 14 * 2**20
PREP_LIMIT = 34 * 2**20
BOUND, ROW, FIRST, SECOND, XA, XB = range(6)
WAITS = {("far", 1): [("r", 0)]}
ORDER = (
    ("far", 0), ("ring1", 0), ("rest", 0), ("far", 1), ("rest", 1), ("ring1", 1), ("ring2", 0), ("ring2", 1), ("ring3", 0), ("ring3", 1),
)
FINE = 16.0
TOP = 32752.0
GROUP_FLOPS = 4400000000


def prepare_kernel(pb, n_dom, n_blk, info, src, rows, cols, tab, dst, sem):
    copy = pltpu.make_async_copy(src, dst, sem)
    copy.start()
    slots, rgroup = rows.shape[1], pb * n_dom
    iota = lambda shape, axis: lax.broadcasted_iota(jnp.int32, shape, axis)
    count, blk, px, py, core = info[0], info[1], info[2], info[3], info[4]

    def position(r):
        kind, y, x = (r >> 2) & 1, (r >> 3) & 3, r >> 5
        first = kind == 0
        u = (jnp.where(first, x, y) - jnp.where(first, px, py)) & 3
        v = (jnp.where(first, y, x) - jnp.where(first, py, px)) & 3
        place = lambda rel: functools.reduce(lambda w, i: jnp.where(rel == REL[i], i, w), range(3), jnp.full_like(rel, 3))
        return ((jnp.where(kind == core, n_dom // 2, 0) + place(u) * 4 + place(v)) * pb + (r & 3)).astype(jnp.float32)

    total = lambda mask, value, axis: jnp.sum(jnp.where(mask, value, 0.0), axis=axis, keepdims=True)
    item = iota((1, slots), 1)
    row = jnp.where(item < count, rows[...] - blk * rgroup, rgroup)
    col = cols[...]
    xcol = jnp.clip((((col >> 7) - blk) & (n_blk - 1)) * pb + (col & (pb - 1)), 0, n_blk * pb - 1).astype(jnp.float32)
    square = (slots, slots)
    down = iota(square, 0)
    turn = lambda v: total(down == iota(square, 1), v, 1)
    row_c, xcol_c = turn(row.astype(jnp.float32)), turn(xcol)
    r_l, r_c = iota((1, rgroup), 1), iota((rgroup, 1), 0)
    halved = lambda n: ((n.astype(jnp.int32) + 1) >> 1).astype(jnp.float32)
    half_l = halved(total(row_c == r_l.astype(jnp.float32), 1.0, 0))
    num_c = total(row == r_c, 1.0, 1)
    ptr_c = total(row < r_c, 1.0, 1)
    half_c = halved(num_c)
    pos_l, pos_c = position(r_l), position(r_c)
    off_c = total(pos_l < pos_c, half_l, 1)
    at = item.astype(jnp.float32)
    hot = (off_c <= at) & (at < off_c + half_c)
    first = jnp.clip(total(hot, ptr_c - 2.0 * off_c, 0) + 2.0 * at, 0.0, slots - 1.0)
    paired = first + 1.0 < total(hot, ptr_c + num_c, 0)
    second = jnp.where(paired, first + 1.0, first)
    down_f = down.astype(jnp.float32)
    of = lambda t: total(down_f == t, xcol_c, 0)
    lines = (
        total(pos_c < at * pb, half_c, 0), total(hot, pos_c, 0), first, second, of(first),
        jnp.where(paired, of(second), float(n_blk * pb)),
    )
    for i, line in enumerate(lines):
        tab[pl.ds(i, 1), :] = line.astype(jnp.int32)
    copy.wait()


def prepare(tiles, tile_rows, tile_cols, tile_counts, pb, n_blk, n_dom):
    slots = tile_rows.shape[0]
    d = lax.axis_index("dom")
    info = jnp.stack([tile_counts[0], lax.axis_index("blk"), d // 8, (d // 2) % 4, d % 2]).astype(jnp.int32)
    smem, vmem = pl.BlockSpec(memory_space=pltpu.SMEM), pl.BlockSpec(memory_space=pltpu.VMEM)
    return pl.pallas_call(
        functools.partial(prepare_kernel, pb, n_dom, n_blk),
        out_shape=[jax.ShapeDtypeStruct((8, slots), jnp.int32), jax.ShapeDtypeStruct(tiles.shape, tiles.dtype)],
        in_specs=[smem, pl.BlockSpec(memory_space=pltpu.HBM), vmem, vmem],
        out_specs=[vmem, vmem],
        scratch_shapes=[pltpu.SemaphoreType.DMA],
        compiler_params=pltpu.CompilerParams(vmem_limit_bytes=PREP_LIMIT),
        cost_estimate=pl.CostEstimate(flops=GROUP_FLOPS, bytes_accessed=1000, transcendentals=0),
        name="prepare",
    )(info, tiles, tile_rows.reshape(1, slots), tile_cols.reshape(1, slots))


def scale_of(msg, groups, g, at=0):
    blk = msg[pl.ds(at + groups * 512, 16), :].astype(jnp.int32).astype(jnp.float32)
    row = lax.broadcasted_iota(jnp.int32, blk.shape, 0)
    e = jnp.sum(jnp.where(row == g, blk, 0.0), axis=0, keepdims=True)
    return jnp.exp2(e * (1 / FINE)) * (1 / TOP)


def loop(count, body):
    if count == 1:
        body(0)
    else:
        lax.fori_loop(0, count, lambda k, _: (body(k), 0)[1], 0)


def kernel(base, total, segs, nin, nwait, outs, carry, tab, tiles, x, *refs):
    ins, out_refs = refs[:nin], refs[nin + nwait : nin + nwait + len(outs)]
    acc, sc = refs[nin + nwait + len(outs) :]
    width = x.shape[-1]

    for first, count, adds, _, _ in segs:

        def begin(k):
            scales = [scale_of(ins[i], n, m + k) for i, n, m in adds]
            for i in range(4):
                value = None
                for (ref, _, m), s in zip(adds, scales):
                    at = pl.ds(pl.multiple_of((m + k) * 512 + i * 128, 128), 128)
                    part = ins[ref][at, :].astype(jnp.int32).astype(jnp.float32) * s
                    value = part if value is None else value + part
                acc[(first + k) * 4 + i] = jnp.zeros(acc.shape[1:], jnp.float32) if value is None else value

        loop(count, begin)

    lo, hi = tab[BOUND, base], tab[BOUND, base + total]

    def body(j, _):
        done = []
        for n in range(UNROLL):
            t = lo + j * UNROLL + n
            row = jnp.where(t < hi, tab[ROW, t] - 4 * base, 4 * total)
            lhs = jnp.concatenate([tiles[tab[FIRST, t]], tiles[tab[SECOND, t]]], axis=1)
            rhs = jnp.concatenate([x[tab[XA, t]], x[tab[XB, t]]], axis=0)
            done.append((row, jnp.dot(lhs, rhs, preferred_element_type=jnp.float32)))
        for row, value in done:
            acc[row] += value
        return 0

    lax.fori_loop(0, (hi - lo + UNROLL - 1) >> (UNROLL.bit_length() - 1), body, 0)

    sublane = lax.broadcasted_iota(jnp.int32, (16, width), 0)
    for o, (_, quant) in enumerate(outs):
        if quant:
            sc[o] = jnp.zeros(sc.shape[1:], jnp.int32)
    for first, count, _, o, place in segs:

        def finish(k):
            out = out_refs[o]
            terms = [acc.at[(first + k) * 4 + i] for i in range(4)]
            if not outs[o][1]:
                for i in range(4):
                    out[pl.ds(i * 128, 128), :] = terms[i][...]
                return
            top = functools.reduce(jnp.maximum, [jnp.max(jnp.abs(t[...]), axis=0, keepdims=True) for t in terms])
            e = jnp.ceil(FINE * jnp.log2(jnp.maximum(top, 1e-30)))
            inv = jnp.exp2(e * (-1 / FINE)) * TOP
            for i in range(4):
                at = pl.ds(pl.multiple_of((place + k) * 512 + i * 128, 128), 128)
                out[at, :] = jnp.round(terms[i][...] * inv).astype(jnp.int32).astype(jnp.int16)
            sc[o] = jnp.where(sublane == place + k, e.astype(jnp.int32), sc[o])

        loop(count, finish)
    for o, (groups, quant) in enumerate(outs):
        if quant:
            out_refs[o][pl.ds(groups * 512, 16), :] = sc[o].astype(jnp.int16)
    for o in range(carry):
        more = ins[nin - carry + o]
        out_refs[o][pl.ds(outs[o][0] * 512 + 16, more.shape[0]), :] = more[...]


def products(name, tab, tiles, x, base, total, segs, ins, outs, wait, carry=0):
    width = x.shape[-1]
    blk = tiles.shape[1]
    smem, vmem = pl.BlockSpec(memory_space=pltpu.SMEM), pl.BlockSpec(memory_space=pltpu.VMEM)
    shapes = [
        jax.ShapeDtypeStruct((n * 512 + 16, width), jnp.int16) if quant else jax.ShapeDtypeStruct((512, width), jnp.float32)
        for n, quant in outs
    ]
    for o in range(carry):
        rows = shapes[o].shape[0] + ins[len(ins) - carry + o].shape[0]
        shapes[o] = jax.ShapeDtypeStruct((rows, width), jnp.int16)
    return pl.pallas_call(
        functools.partial(kernel, base, total, segs, len(ins), len(wait), outs, carry),
        out_shape=shapes,
        in_specs=[smem] + [vmem] * (2 + len(ins)) + [pl.BlockSpec(memory_space=pl.ANY)] * len(wait),
        out_specs=[vmem] * len(outs),
        scratch_shapes=[
            pltpu.VMEM((4 * total + 1, blk, width), jnp.float32),
            pltpu.VMEM((len(outs), 16, width), jnp.int32),
        ],
        compiler_params=pltpu.CompilerParams(vmem_limit_bytes=VMEM_LIMIT),
        cost_estimate=pl.CostEstimate(flops=total * GROUP_FLOPS, bytes_accessed=1000, transcendentals=0),
        name=name,
    )(tab, tiles, x, *ins, *wait)


def join_kernel(n, nwait, *refs):
    out, at = refs[-1], 0
    for part in refs[:n]:
        out[pl.ds(at, part.shape[0])] = part[...]
        at += part.shape[0]
    out[pl.ds(at, out.shape[0] - at)] = jnp.zeros((out.shape[0] - at, *out.shape[1:]), out.dtype)


def join(name, parts, blk, wait):
    parts = [p.reshape(-1, blk, p.shape[-1]) for p in parts]
    total = sum(p.shape[0] for p in parts)
    return pl.pallas_call(
        functools.partial(join_kernel, len(parts), len(wait)),
        out_shape=jax.ShapeDtypeStruct((total + 1, *parts[0].shape[1:]), parts[0].dtype),
        in_specs=[pl.BlockSpec(memory_space=pltpu.VMEM)] * len(parts) + [pl.BlockSpec(memory_space=pl.ANY)] * len(wait),
        out_specs=pl.BlockSpec(memory_space=pltpu.VMEM),
        compiler_params=pltpu.CompilerParams(vmem_limit_bytes=VMEM_LIMIT),
        cost_estimate=pl.CostEstimate(flops=1000, bytes_accessed=1000, transcendentals=0),
        name=name,
    )(*parts, *wait)


def add_up_kernel(n, ngot, *refs):
    owns, got, out = refs[:n], refs[n : n + ngot], refs[-1]
    left = 0
    for j, own in enumerate(owns):
        right, begin = left + own.shape[1], (n - 1 - j) * 528
        scales = [scale_of(m, 1, 0, begin) for m in got]
        for i in range(own.shape[0] // 128):
            value = own[i * 128 : (i + 1) * 128, :]
            for m, s in zip(got, scales):
                value = value + m[pl.ds(begin + i * 128, 128), :].astype(jnp.int32).astype(jnp.float32) * s
            out[i * 128 : (i + 1) * 128, left:right] = value
        left = right


def add_up(owns, got, wait):
    rows, width = owns[0].shape[0], sum(own.shape[1] for own in owns)
    vmem = pl.BlockSpec(memory_space=pltpu.VMEM)
    return pl.pallas_call(
        functools.partial(add_up_kernel, len(owns), len(got)),
        out_shape=jax.ShapeDtypeStruct((rows, width), jnp.float32),
        in_specs=[vmem] * (len(owns) + len(got)) + [pl.BlockSpec(memory_space=pl.ANY)] * len(wait),
        out_specs=vmem,
        compiler_params=pltpu.CompilerParams(vmem_limit_bytes=VMEM_LIMIT),
        name="add_up",
    )(*owns, *got, *wait)


def shards(tiles, tile_rows, tile_cols, tile_counts, loads_in):
    blk, loads = tiles.shape[1], loads_in.shape[1]
    pb = loads_in.shape[0] // blk
    n_blk, n_dom = lax.axis_size("blk"), lax.axis_size("dom")
    tab, tiles = prepare(tiles, tile_rows, tile_cols, tile_counts, pb, n_blk, n_dom)
    edges = [loads * sum(SPLIT[:j]) // sum(SPLIT) for j in range(CHUNKS + 1)]

    place = lambda x, y, c: (x % 4 * 4 + y % 4) * 2 + c
    every = [(x, y, c) for x in range(4) for y in range(4) for c in range(2)]
    pair = [(place(x, y, c), place(x, y, 1 - c)) for x, y, c in every]
    along = lambda k, axis: [
        (place(x, y, c), place(x + k, y, c) if c == axis else place(x, y + k, c)) for x, y, c in every
    ]
    send = lambda value, pairs: lax.ppermute(value, "dom", pairs)

    ring = lambda k: [(i, (i - k) % n_blk) for i in range(n_blk)]
    parts = []
    for j in range(CHUNKS):
        part = loads_in[:, edges[j] : edges[j + 1]]
        others = [lax.ppermute(part, "blk", ring(k)) for k in (1, n_blk - 1, *range(2, n_blk - 1))]
        others.insert(n_blk - 2, others.pop(1))
        parts.append([part, *others])
    last, xs = [], {}
    kept = [{} for _ in range(CHUNKS)]
    late, owns = [], []

    def run(name, j, **how):
        wait = [v for key, i in WAITS.get((name, j), ()) for v in kept[i][key]]
        if j not in xs:
            xs[j] = join(f"join_{j}", parts[j], blk, list(last))
        value = products(f"{name}_{j}", tab, tiles, xs[j], wait=[*last, *wait], **how)
        last[:] = [value[-1]]
        return value

    def far(j, k):
        [a] = run("far", j, base=0, total=4, segs=[(0, 4, [], 0, 0)], ins=[], outs=[(4, True)])
        k["p1"] = send(a, pair)

    def ring1(j, k):
        h1, h2 = run(
            "ring1", j, base=16, total=4, ins=[k["p1"]], outs=[(2, True), (2, True)],
            segs=[(0, 2, [(0, 4, 0)], 0, 0), (2, 2, [(0, 4, 2)], 1, 0)],
        )
        k["r"] = send(h1, along(1, 0)), send(h2, along(-1, 0))

    def rest(j, k):
        [a] = run("rest", j, base=4, total=12, segs=[(0, 12, [], 0, 0)], ins=[], outs=[(12, True)])
        k["p2"] = [send(a, pair)]

    def ring2(j, k):
        m1, m2 = run(
            "ring2", j, base=20, total=8, ins=[*k["p2"], *k["r"]], outs=[(4, True), (4, True)],
            segs=[
                (0, 2, [(0, 12, 0), (1, 2, 0)], 0, 0),
                (2, 2, [(0, 12, 2)], 0, 2),
                (4, 2, [(0, 12, 4)], 1, 0),
                (6, 2, [(0, 12, 6), (2, 2, 0)], 1, 2),
            ],
        )
        k["n"] = send(m1, along(1, 0)), send(m2, along(-1, 0))

    def ring3(j, k):
        *t, own = run(
            "ring3", j, base=28, total=4, ins=[*k["p2"], *k["n"], *late], outs=[(1, True), (1, True), (1, True), (1, False)],
            segs=[(g, 1, [(0, 12, 8 + g), (1, 4, g), (2, 4, g)], g, 0) for g in range(4)], carry=len(late),
        )
        late[:] = t
        owns.append(own)

    for step, j in ORDER:
        dict(far=far, ring1=ring1, rest=rest, ring2=ring2, ring3=ring3)[step](j, kept[j])
    got = [send(t, along(k, 1)) for t, k in zip(late, (2, 1, -1))]
    return add_up(owns, got, last)


def solution(mesh):
    in_specs = (
        P(("blk", "dom"), None, None),
        P(("blk", "dom")),
        P(("blk", "dom")),
        P(("blk", "dom")),
        P(("blk", "dom"), None),
    )
    out_specs = P(("blk", "dom"), None)
    return jax.shard_map(shards, mesh=mesh, in_specs=in_specs, out_specs=out_specs, check_vma=False)
```
